32 devices in a mesh: groups: 2 (over y), ctx: 4 (over z), kv: 2 (over x), khalf: 2 (over core).
Axes of the slice: x: 2, y: 2, z: 4, core: 2. Of those that a mesh axis runs over, the one named last changes fastest.
Arguments:
- queries: bfloat16 [256, 8192], P(('groups', 'ctx'), 'kv'), parts along dimension 0, may hold values from -100 to 100
- cache_keys: bfloat16 [49152, 1024], P(('groups', 'ctx', 'khalf'), 'kv'), parts along dimension 0, may hold values from -7 to 7
- cache_values: bfloat16 [49152, 1024], P(('groups', 'ctx', 'khalf'), 'kv'), parts along dimension 0, may hold values from -6 to 6
- new_keys: bfloat16 [256, 1024], P(('groups', 'ctx'), 'kv'), parts along dimension 0, may hold values from -10 to 10
- new_values: bfloat16 [256, 1024], P(('groups', 'ctx'), 'kv'), parts along dimension 0, may hold values from -6 to 6
- cache_blocks: int32 [2], P('groups'), parts along dimension 0, may hold values from 48 to 192
- residual: bfloat16 [256, 8192], P('groups', ('ctx', 'khalf')), parts along dimension 0, may hold values from -20 to 20
- norm_gain: float32 [8192], P(('ctx', 'khalf')), may hold values from 0.1 to 1.9
- out_weight: bfloat16 [8192, 8192], P('kv', ('ctx', 'khalf')), may hold values from -0.0625 to 0.0625
- gate_up: bfloat16 [8192, 2, 14336], P(('ctx', 'khalf'), None, 'kv'), may hold values from -0.0625 to 0.0625
- down_weight: bfloat16 [14336, 8192], P('kv', ('ctx', 'khalf')), may hold values from -0.046875 to 0.046875
Outputs:
- layer_out: bfloat16 [256, 8192], P(('groups', 'kv'), ('ctx', 'khalf')), parts along dimension 0
The draws below stay inside these ranges and needn't reach their ends.
There are 2 independent parts, one for each index of `groups`. The reference program is written for one: setup_inputs(seed, part) draws one part's arguments, and reference() takes and returns one part's arrays. A program takes and returns all parts, laid end to end along the dimension named above; an argument that names none is the same for every part. Nothing has to cross between parts.
Inputs may be any that keep to these rules, and one draw needn't show every extreme that they name: The first 128 * cache_blocks[0] cached positions are valid.
All inputs are finite; a program needn't handle non-finite values.
Results may differ from the reference program's by a relative error of at most 0.019.
Values may be sent and summed in bfloat16 or wider, within the bound.
A program may use at most 128 MiB of HBM per device.

```python
import jax
import jax.numpy as jnp
from jax import lax

D = 8192
HQ = 64
KVH = 8
DH = 128
FF = 14336
NEW = 128
BLOCK = 128
CACHE = 24576


def key_table(key):
    key_base = jax.random.truncated_normal(jax.random.fold_in(key, 11), -4.0, 4.0, (CACHE, KVH * DH), jnp.float32) * 1.7
    return key_base


def draw_cache_keys(key, part):
    key_base = key_table(key)
    return key_base.astype(jnp.bfloat16)


def draw_queries(key, part):
    query_key = jax.random.fold_in(key, 13)
    drawn = jax.random.truncated_normal(query_key, -4.0, 4.0, (NEW, HQ * DH), jnp.float32) * 1.7
    return drawn.astype(jnp.bfloat16)


def draw_residual(key, part):
    column = jnp.arange(D, dtype=jnp.float32) / D
    rough = jax.random.uniform(jax.random.fold_in(key, 21), (D,), jnp.float32, 0.7, 1.4)
    row_scale = 10.0 ** (0.5 * jax.random.uniform(jax.random.fold_in(key, 22), (NEW, 1), jnp.float32) - 0.25)
    noise = jax.random.truncated_normal(jax.random.fold_in(key, 23), -4.0, 4.0, (NEW, D), jnp.float32)
    column_scale = 10.0 ** (0.5 * column - 0.25)
    return (noise * column_scale * rough * row_scale).astype(jnp.bfloat16)


def steps_of(own_key, extent, shards, least, top_value):
    factor_of = 1.0
    for axis_at, shards_of in shards:
        draws = jax.random.uniform(jax.random.fold_in(jax.random.fold_in(own_key, 6), axis_at), (shards_of,), jnp.float32, least / len(shards), top_value / len(shards))
        factor_of = factor_of * jnp.repeat(jnp.exp(draws), extent[axis_at] // shards_of).reshape((-1,) + (1,) * (len(extent) - 1 - axis_at))
    return factor_of


def normal_values(own_key, shape, scale, bound, split=(), kind=jnp.bfloat16):
    result = scale * jax.random.normal(own_key, shape, jnp.float32)
    if split:
        result = result * steps_of(own_key, shape, split, -0.22, 0.18)
    return jnp.clip(result, -bound, bound).astype(kind)


def setup_inputs(seed: int = 0, part: int = 0) -> dict:
    keys = jax.random.split(jax.random.key(seed), 12)
    own_keys = jax.random.split(jax.random.fold_in(keys[11], part), 12)
    return {
        "queries": draw_queries(jax.random.fold_in(jax.random.fold_in(keys[11], part), 71), part),
        "cache_keys": draw_cache_keys(jax.random.fold_in(jax.random.fold_in(keys[11], part), 71), part),
        "cache_values": normal_values(own_keys[2], (CACHE, KVH * DH), 1.0, 6.0, ((0, 8), (1, 2))),
        "new_keys": normal_values(own_keys[3], (NEW, KVH * DH), 2.5, 10.0, ((0, 4), (1, 2))),
        "new_values": normal_values(own_keys[4], (NEW, KVH * DH), 1.0, 6.0, ((0, 4), (1, 2))),
        "cache_blocks": jax.random.randint(own_keys[5], (1,), CACHE // (4 * BLOCK), CACHE // BLOCK + 1).astype(jnp.int32),
        "residual": draw_residual(jax.random.fold_in(jax.random.fold_in(keys[11], part), 71), part),
        "norm_gain": jnp.clip(1.0 + 0.18 * jax.random.normal(keys[7], (D,), jnp.float32), 0.1, 1.9),
        "out_weight": normal_values(keys[8], (HQ * DH, D), (HQ * DH) ** -0.5, 0.0625, ((0, 2), (1, 8))),
        "gate_up": normal_values(keys[9], (D, 2, FF), D ** -0.5, 0.0625, ((0, 8), (2, 2))),
        "down_weight": normal_values(keys[10], (FF, D), FF ** -0.5, 0.046875, ((0, 2), (1, 8))),
    }


NEG = -1e+30

def reference(queries, cache_keys, cache_values, new_keys, new_values, cache_blocks, residual, norm_gain, out_weight, gate_up, down_weight):
    group_size = HQ // KVH
    valid_length = cache_blocks[0] * BLOCK
    cache_mask = jnp.arange(CACHE, dtype=jnp.int32) < valid_length
    token_index = jnp.arange(NEW, dtype=jnp.int32)
    self_mask = token_index[None, :] <= token_index[:, None]
    full_mask = jnp.concatenate([jnp.broadcast_to(cache_mask[None, :], (NEW, CACHE)), self_mask], axis=1)

    def one_head(head):
        column = (head // group_size * DH).astype(jnp.int32)
        query_cols = lax.dynamic_slice_in_dim(queries, (head * DH).astype(jnp.int32), DH, 1)
        key_rows = jnp.concatenate([lax.dynamic_slice_in_dim(cache_keys, column, DH, 1), lax.dynamic_slice_in_dim(new_keys, column, DH, 1)], axis=0)
        value_rows = jnp.concatenate([lax.dynamic_slice_in_dim(cache_values, column, DH, 1), lax.dynamic_slice_in_dim(new_values, column, DH, 1)], axis=0)
        scores = jnp.dot(query_cols, key_rows.T, preferred_element_type=jnp.float32) * DH ** (-0.5)
        scores = jnp.where(full_mask, scores, NEG)
        peak_score = lax.optimization_barrier(jnp.max(scores, axis=1, keepdims=True))
        weights = jnp.where(full_mask, jnp.exp(scores - peak_score), 0.0)
        weight_sum = lax.optimization_barrier(jnp.sum(weights, axis=1, keepdims=True))
        summed = jnp.dot(weights.astype(jnp.bfloat16), value_rows, preferred_element_type=jnp.float32)
        return (summed / weight_sum).astype(jnp.bfloat16)
    heads = lax.map(one_head, jnp.arange(HQ, dtype=jnp.int32))
    attention = jnp.transpose(heads, (1, 0, 2)).reshape(NEW, HQ * DH)
    projected = jnp.dot(attention, out_weight, preferred_element_type=jnp.float32)
    hidden_state = (residual.astype(jnp.float32) + projected).astype(jnp.bfloat16)
    values32 = hidden_state.astype(jnp.float32)
    mean_square = lax.optimization_barrier(jnp.mean(values32 * values32, axis=1, keepdims=True))
    normed = (values32 * lax.rsqrt(mean_square + 1e-05) * norm_gain).astype(jnp.bfloat16)
    both = jnp.dot(normed, gate_up.reshape(D, 2 * FF), preferred_element_type=jnp.float32)
    activated = (jax.nn.silu(both[:, :FF]) * both[:, FF:]).astype(jnp.bfloat16)
    down = jnp.dot(activated, down_weight, preferred_element_type=jnp.float32)
    return (values32 + down).astype(jnp.bfloat16)
```

```python
import functools

import jax
import jax.numpy as jnp
from jax import lax
from jax.experimental import pallas as pl
from jax.experimental.pallas import tpu as pltpu
from jax.sharding import PartitionSpec as P

HQ = 64
DH = 128
BLOCK = 128

NEG = -1e30
EPSILON = 1e-05
MESH = pl.DeviceIdType.MESH
VMEM_LIMIT = 56 * 1024 * 1024


def peers(axis):
    n = lax.axis_size(axis)
    me = lax.axis_index(axis)
    return n, me, [lax.rem(me + o, n) for o in range(1, n)], [
        lax.rem(me + n - o, n) for o in range(1, n)
    ]


def meet(devices):
    barrier = pltpu.get_barrier_semaphore()
    for device in devices:
        pl.semaphore_signal(barrier, inc=1, device_id=device, device_id_type=MESH)
    pl.semaphore_wait(barrier, len(devices))


def remote(src, dst, send, recv, device):
    return pltpu.make_async_remote_copy(
        src_ref=src, dst_ref=dst, send_sem=send, recv_sem=recv, device_id=device, device_id_type=MESH
    )


def vmem(count):
    return [pl.BlockSpec(memory_space=pltpu.VMEM)] * count


def params(collective_id):
    return pltpu.CompilerParams(
        collective_id=collective_id, has_side_effects=True, vmem_limit_bytes=VMEM_LIMIT
    )


def gather_queries_kernel(q_ref, o_ref, zs, zr, ks, kr, own):
    n, me, after, before = peers("ctx")
    k = lax.axis_index("khalf")
    sibling = {"khalf": 1 - k}
    meet([{"ctx": c} for c in after] + [sibling])
    half = q_ref.shape[0] // 2
    mine = pl.ds(k * half, half)
    other = pl.ds((1 - k) * half, half)
    out = [
        remote(q_ref.at[mine], o_ref.at[me, mine], zs.at[i], zr.at[i], {"ctx": c})
        for i, c in enumerate(after)
    ]
    for copy in out:
        copy.start()
    local = pltpu.make_async_copy(q_ref, o_ref.at[me], own)
    local.start()
    on = []
    for i, c in enumerate(before):
        remote(o_ref.at[c, mine], o_ref.at[c, mine], zs.at[i], zr.at[i], sibling).wait_recv()
        copy = remote(o_ref.at[c, mine], o_ref.at[c, mine], ks.at[i], kr.at[i], sibling)
        copy.start()
        on.append(copy)
    for i, c in enumerate(before):
        remote(o_ref.at[c, other], o_ref.at[c, other], ks.at[i], kr.at[i], sibling).wait_recv()
    local.wait()
    for copy in out + on:
        copy.wait_send()


def gather_queries(q):
    n = lax.axis_size("ctx")
    sems = pltpu.SemaphoreType.DMA((max(n - 1, 1),))
    return pl.pallas_call(
        gather_queries_kernel,
        out_shape=jax.ShapeDtypeStruct((n,) + q.shape, q.dtype),
        in_specs=vmem(1),
        out_specs=vmem(1)[0],
        scratch_shapes=[sems] * 4 + [pltpu.SemaphoreType.DMA],
        compiler_params=params(0),
        name="gather_queries",
    )(q)


def to_rows(block):
    shape = block.shape
    flat = (shape[0] * shape[1] * shape[2], shape[3])
    if shape[2] % 16 == 0:
        return block.reshape(flat)
    return block.astype(jnp.float32).reshape(flat).astype(block.dtype)


def attend_kernel(chunk, place_ref, q_ref, k_ref, v_ref, nk_ref, nv_ref, acc_ref, st_ref):
    ctx, heads, rows, width = q_ref.shape
    count = ctx * heads * rows
    q = to_rows(q_ref[...])
    scale = width ** (-0.5)
    cached = place_ref[0]
    new_start = place_ref[1]
    use_new = place_ref[2]
    keys = k_ref.shape[0]

    def scored(block, usable):
        s = lax.dot_general(block, q, (((1,), (1,)), ((), ())), preferred_element_type=jnp.float32)
        s = jnp.where(usable, s * scale, NEG)
        return s

    def update(state, s, usable, values):
        m, l, acc = state
        m_new = jnp.maximum(m, jnp.max(s, axis=0, keepdims=True))
        p = jnp.where(usable, jnp.exp(s - m_new), 0.0)
        alpha = jnp.exp(m - m_new)
        l = l * alpha + jnp.sum(p, axis=0, keepdims=True)
        pv = lax.dot_general(
            values, p.astype(jnp.bfloat16), (((0,), (0,)), ((), ())), preferred_element_type=jnp.float32
        )
        return m_new, l, acc * alpha + pv

    state = (
        jnp.full((1, count), NEG, jnp.float32),
        jnp.zeros((1, count), jnp.float32),
        jnp.zeros((width, count), jnp.float32),
    )
    for start in range(0, keys, chunk):
        usable = lax.broadcasted_iota(jnp.int32, (chunk, 1), 0) + start < cached
        s = scored(k_ref[start : start + chunk, :], usable)
        state = update(state, s, usable, v_ref[start : start + chunk, :])
    new_count = nk_ref.shape[0]
    lane = lax.broadcasted_iota(jnp.int32, (1, count), 1)
    token = lane // (heads * rows) * rows + lane % rows
    key_at = lax.broadcasted_iota(jnp.int32, (new_count, 1), 0) + new_start
    usable = (key_at <= token) & (use_new > 0)
    s = scored(nk_ref[...], usable)
    m, l, acc = update(state, s, usable, nv_ref[...])
    acc_ref[...] = acc[None]
    st_ref[...] = jnp.zeros(st_ref.shape, jnp.float32)
    st_ref[0, 0:1, :] = m
    st_ref[0, 1:2, :] = l


def attend(q_all, keys, values, new_keys, new_values, place):
    ctx, heads, rows, width = q_all.shape
    groups = keys.shape[1] // width
    size = heads // groups
    count = ctx * size * rows
    length = keys.shape[0]
    chunk = next(c for c in (512, 256, 128, length) if length % c == 0)
    column = lambda n: pl.BlockSpec((n, width), lambda g: (0, g))
    return pl.pallas_call(
        functools.partial(attend_kernel, chunk),
        grid=(groups,),
        out_shape=(
            jax.ShapeDtypeStruct((groups, width, count), jnp.float32),
            jax.ShapeDtypeStruct((groups, 8, count), jnp.float32),
        ),
        in_specs=[
            pl.BlockSpec(memory_space=pltpu.SMEM),
            pl.BlockSpec((ctx, size, rows, width), lambda g: (0, g, 0, 0)),
            column(length),
            column(length),
            column(new_keys.shape[0]),
            column(new_keys.shape[0]),
        ],
        out_specs=(
            pl.BlockSpec((1, width, count), lambda g: (g, 0, 0)),
            pl.BlockSpec((1, 8, count), lambda g: (g, 0, 0)),
        ),
        compiler_params=pltpu.CompilerParams(vmem_limit_bytes=VMEM_LIMIT),
        name="attend",
    )(place, q_all, keys, values, new_keys, new_values)


def merge_kernel(
    acc_ref, st_ref, o_ref,
    sib_st, chip_st, ctx_st, part, sib_part, mine_part, ctx_part,
    s_st, r_st, s_z, r_z, s_p, r_p, s_a, r_a, s_g, r_g, s_k, r_k,
):
    n, me, after, before = peers("ctx")
    k = lax.axis_index("khalf")
    sibling = {"khalf": 1 - k}
    meet([{"ctx": c} for c in after] + [sibling])
    groups, width, count = acc_ref.shape
    _, heads, rows, _ = part.shape
    size = heads // groups
    half = heads // 2

    def stat_of(ref, at=()):
        return ref[at + (slice(None), slice(0, 1))], ref[at + (slice(None), slice(1, 2))]

    def joined(a, b):
        m = jnp.maximum(a[0], b[0])
        return m, a[1] * jnp.exp(a[0] - m) + b[1] * jnp.exp(b[0] - m)

    copy = remote(st_ref, sib_st, s_st, r_st, sibling)
    copy.start()
    copy.wait()
    own = stat_of(st_ref)
    chip = joined(own, stat_of(sib_st))
    chip_st[...] = jnp.zeros(chip_st.shape, jnp.float32)
    chip_st[:, 0:1, :] = chip[0]
    chip_st[:, 1:2, :] = chip[1]
    copies = [
        remote(chip_st, ctx_st.at[i], s_z.at[i], r_z.at[i], {"ctx": c}) for i, c in enumerate(after)
    ]
    for copy in copies:
        copy.start()
    total = chip
    for i, copy in enumerate(copies):
        copy.wait()
        total = joined(total, stat_of(ctx_st, (i,)))
    factor = jnp.exp(own[0] - total[0]) / total[1]
    for g in range(groups):
        scaled = jnp.transpose(acc_ref[g] * factor[g])
        part[:, g * size : (g + 1) * size] = scaled.reshape(n, size, rows, width).astype(part.dtype)
    copy = remote(part.at[:, pl.ds((1 - k) * half, half)], sib_part, s_p, r_p, sibling)
    copy.start()
    copy.wait()
    for c in range(n):
        mine_part[c] = (
            part[c, pl.ds(k * half, half)].astype(jnp.float32) + sib_part[c].astype(jnp.float32)
        ).astype(part.dtype)
    copies = [
        remote(mine_part.at[c], ctx_part.at[i], s_a.at[i], r_a.at[i], {"ctx": c})
        for i, c in enumerate(after)
    ]
    for copy in copies:
        copy.start()
    summed = mine_part[me].astype(jnp.float32)
    for i, copy in enumerate(copies):
        copy.wait()
        summed = summed + ctx_part[i].astype(jnp.float32)
    mine = pl.ds(k * half, half)
    other = pl.ds((1 - k) * half, half)
    o_ref[me, mine] = summed.astype(o_ref.dtype)
    out = [
        remote(o_ref.at[me, mine], o_ref.at[me, mine], s_g.at[i], r_g.at[i], {"ctx": c})
        for i, c in enumerate(after)
    ]
    on = [remote(o_ref.at[me, mine], o_ref.at[me, mine], s_k.at[n - 1], r_k.at[n - 1], sibling)]
    for copy in out + on:
        copy.start()
    for i, c in enumerate(before):
        remote(o_ref.at[c, mine], o_ref.at[c, mine], s_g.at[i], r_g.at[i], sibling).wait_recv()
        copy = remote(o_ref.at[c, mine], o_ref.at[c, mine], s_k.at[i], r_k.at[i], sibling)
        copy.start()
        on.append(copy)
    for i, c in enumerate(before + [me]):
        remote(o_ref.at[c, other], o_ref.at[c, other], s_k.at[i], r_k.at[i], sibling).wait_recv()
    for copy in out + on:
        copy.wait_send()


def merge(acc, stats, heads, rows):
    n = lax.axis_size("ctx")
    width = acc.shape[1]
    f32 = lambda *shape: pltpu.VMEM(shape, jnp.float32)
    b16 = lambda *shape: pltpu.VMEM(shape, jnp.bfloat16)
    one = pltpu.SemaphoreType.DMA
    many = pltpu.SemaphoreType.DMA((n,))
    return pl.pallas_call(
        merge_kernel,
        out_shape=jax.ShapeDtypeStruct((n, heads, rows, width), jnp.bfloat16),
        in_specs=vmem(2),
        out_specs=vmem(1)[0],
        scratch_shapes=[
            f32(*stats.shape), f32(*stats.shape), f32(max(n - 1, 1), *stats.shape),
            b16(n, heads, rows, width), b16(n, heads // 2, rows, width),
            b16(n, heads // 2, rows, width), b16(max(n - 1, 1), heads // 2, rows, width),
            one, one, many, many, one, one, many, many, many, many, many, many,
        ],
        compiler_params=params(1),
        name="merge",
    )(acc, stats)


def norm_kernel(
    total_width, p_ref, r_ref, g_ref, h_ref, n_ref, got, sq, sq_got, s_x, r_x, s_q, r_q
):
    n, me, after, _ = peers("ctx")
    k = lax.axis_index("khalf")
    _, _, across, _ = peers("kv")
    partners = [{"ctx": c} for c in after]
    partners += [{"ctx": c, "khalf": 1 - k} for c in [me] + after]
    meet([{"kv": c} for c in across] + partners)
    copies = [
        remote(p_ref, got.at[i], s_x.at[i], r_x.at[i], {"kv": c}) for i, c in enumerate(across)
    ]
    for copy in copies:
        copy.start()
    summed = p_ref[...].astype(jnp.float32)
    for i, copy in enumerate(copies):
        copy.wait()
        summed = summed + got[i].astype(jnp.float32)
    hidden = (r_ref[...].astype(jnp.float32) + summed).astype(h_ref.dtype)
    h_ref[...] = hidden
    values = hidden.astype(jnp.float32)
    squares = values * values
    rows, columns = values.shape
    lanes = squares[:, 0:128]
    for at in range(128, columns, 128):
        lanes = lanes + squares[:, at : at + 128]
    row = jnp.sum(jnp.transpose(lanes), axis=0, keepdims=True)
    sq[...] = jnp.broadcast_to(row, sq.shape)
    copies = [
        remote(sq, sq_got.at[i], s_q.at[i], r_q.at[i], device) for i, device in enumerate(partners)
    ]
    for copy in copies:
        copy.start()
    total = row
    for i, copy in enumerate(copies):
        copy.wait()
        total = total + sq_got[i, 0:1, :]
    factor = lax.rsqrt(total / total_width + EPSILON)
    column = jnp.transpose(jnp.broadcast_to(factor, (128, rows)))[:, 0:1]
    n_ref[...] = (values * column * g_ref[...]).astype(n_ref.dtype)


def norm(partial, residual, gain, total_width):
    rows, columns = partial.shape
    devices = lax.axis_size("ctx") * 2
    across = lax.axis_size("kv")
    shape = jax.ShapeDtypeStruct((rows, columns), jnp.bfloat16)
    many = lambda n: pltpu.SemaphoreType.DMA((max(n, 1),))
    return pl.pallas_call(
        functools.partial(norm_kernel, total_width),
        out_shape=(shape, shape),
        in_specs=vmem(3),
        out_specs=tuple(vmem(2)),
        scratch_shapes=[
            pltpu.VMEM((max(across - 1, 1), rows, columns), jnp.bfloat16),
            pltpu.VMEM((8, rows), jnp.float32),
            pltpu.VMEM((devices - 1, 8, rows), jnp.float32),
            many(across - 1), many(across - 1), many(devices - 1), many(devices - 1),
        ],
        compiler_params=params(2),
        name="norm",
    )(partial, residual, gain)


def finish_kernel(p_ref, h_ref, o_ref, got, s_x, r_x):
    n, me, across, _ = peers("kv")
    meet([{"kv": c} for c in across])
    copies = [
        remote(p_ref.at[c], got.at[i], s_x.at[i], r_x.at[i], {"kv": c}) for i, c in enumerate(across)
    ]
    for copy in copies:
        copy.start()
    summed = p_ref[me].astype(jnp.float32)
    for i, copy in enumerate(copies):
        copy.wait()
        summed = summed + got[i].astype(jnp.float32)
    o_ref[...] = (h_ref[me].astype(jnp.float32) + summed).astype(o_ref.dtype)


def finish(partial, hidden):
    n = lax.axis_size("kv")
    rows, columns = partial.shape
    block = (n, rows // n, columns)
    many = pltpu.SemaphoreType.DMA((max(n - 1, 1),))
    return pl.pallas_call(
        finish_kernel,
        out_shape=jax.ShapeDtypeStruct(block[1:], jnp.bfloat16),
        in_specs=vmem(2),
        out_specs=vmem(1)[0],
        scratch_shapes=[pltpu.VMEM((max(n - 1, 1),) + block[1:], jnp.bfloat16), many, many],
        compiler_params=params(3),
        name="finish",
    )(partial.reshape(block), hidden.reshape(block))


def on_device(
    queries,
    cache_keys,
    cache_values,
    new_keys,
    new_values,
    cache_blocks,
    residual,
    norm_gain,
    out_weight,
    gate_up,
    down_weight,
):
    rows = queries.shape[0]
    heads = queries.shape[1] // DH
    ctx = lax.axis_index("ctx")
    khalf = lax.axis_index("khalf")
    length = cache_keys.shape[0]
    start = (ctx * lax.axis_size("khalf") + khalf) * length
    place = jnp.stack(
        [cache_blocks[0] * BLOCK - start, ctx * rows, jnp.where(khalf == 0, 1, 0)]
    ).astype(jnp.int32)
    local_queries = queries.reshape(rows, heads, DH).transpose(1, 0, 2)
    q_all = gather_queries(local_queries)
    acc, stats = attend(q_all, cache_keys, cache_values, new_keys, new_values, place)
    attention = merge(acc, stats, heads, rows)
    tokens = attention.shape[0] * rows
    attention = attention.transpose(0, 2, 1, 3).reshape(tokens, heads * DH)
    partial_rows = jnp.dot(attention, out_weight, preferred_element_type=jnp.float32)
    total_width = out_weight.shape[1] * lax.axis_size("ctx") * lax.axis_size("khalf")
    hidden_state, normed = norm(
        partial_rows.astype(jnp.bfloat16), residual, norm_gain[None, :], total_width
    )
    both = jnp.einsum("tk,ksn->tsn", normed, gate_up, preferred_element_type=jnp.float32)
    both = lax.psum_scatter(
        both.astype(jnp.bfloat16), ("ctx", "khalf"), scatter_dimension=0, tiled=True
    ).astype(jnp.float32)
    activated = (jax.nn.silu(both[:, 0]) * both[:, 1]).astype(jnp.bfloat16)
    partial_out = jnp.dot(
        lax.all_gather(activated, ("ctx", "khalf"), axis=0, tiled=True),
        down_weight,
        preferred_element_type=jnp.float32,
    )
    return finish(partial_out.astype(jnp.bfloat16), hidden_state)


def solution(mesh):
    in_specs = (
        P(("groups", "ctx"), "kv"),
        P(("groups", "ctx", "khalf"), "kv"),
        P(("groups", "ctx", "khalf"), "kv"),
        P(("groups", "ctx"), "kv"),
        P(("groups", "ctx"), "kv"),
        P("groups"),
        P("groups", ("ctx", "khalf")),
        P(("ctx", "khalf")),
        P("kv", ("ctx", "khalf")),
        P(("ctx", "khalf"), None, "kv"),
        P("kv", ("ctx", "khalf")),
    )
    out_specs = P(("groups", "kv"), ("ctx", "khalf"))
    return jax.shard_map(
        on_device, mesh=mesh, in_specs=in_specs, out_specs=out_specs, check_vma=False
    )
```

```python
import functools

import jax
import jax.numpy as jnp
from jax import lax
from jax.experimental import pallas as pl
from jax.experimental.pallas import tpu as pltpu
from jax.sharding import PartitionSpec as P

HQ = 64
DH = 128
BLOCK = 128

NEG = -1e30
EPSILON = 1e-05
MESH = pl.DeviceIdType.MESH
VMEM_LIMIT = 56 * 1024 * 1024


def peers(axis):
    n = lax.axis_size(axis)
    me = lax.axis_index(axis)
    return n, me, [lax.rem(me + o, n) for o in range(1, n)], [
        lax.rem(me + n - o, n) for o in range(1, n)
    ]


def meet(devices):
    barrier = pltpu.get_barrier_semaphore()
    for device in devices:
        pl.semaphore_signal(barrier, inc=1, device_id=device, device_id_type=MESH)
    pl.semaphore_wait(barrier, len(devices))


def remote(src, dst, send, recv, device):
    return pltpu.make_async_remote_copy(
        src_ref=src, dst_ref=dst, send_sem=send, recv_sem=recv, device_id=device, device_id_type=MESH
    )


def vmem(count):
    return [pl.BlockSpec(memory_space=pltpu.VMEM)] * count


def params(collective_id):
    return pltpu.CompilerParams(
        collective_id=collective_id, has_side_effects=True, vmem_limit_bytes=VMEM_LIMIT
    )


def gather_queries_kernel(q_ref, o_ref, zs, zr, ks, kr, own):
    n, me, after, before = peers("ctx")
    k = lax.axis_index("khalf")
    sibling = {"khalf": 1 - k}
    meet([{"ctx": c} for c in after] + [sibling])
    half = q_ref.shape[0] // 2
    mine = pl.ds(k * half, half)
    other = pl.ds((1 - k) * half, half)
    out = [
        remote(q_ref.at[mine], o_ref.at[me, mine], zs.at[i], zr.at[i], {"ctx": c})
        for i, c in enumerate(after)
    ]
    for copy in out:
        copy.start()
    local = pltpu.make_async_copy(q_ref, o_ref.at[me], own)
    local.start()
    on = []
    for i, c in enumerate(before):
        remote(o_ref.at[c, mine], o_ref.at[c, mine], zs.at[i], zr.at[i], sibling).wait_recv()
        copy = remote(o_ref.at[c, mine], o_ref.at[c, mine], ks.at[i], kr.at[i], sibling)
        copy.start()
        on.append(copy)
    for i, c in enumerate(before):
        remote(o_ref.at[c, other], o_ref.at[c, other], ks.at[i], kr.at[i], sibling).wait_recv()
    local.wait()
    for copy in out + on:
        copy.wait_send()


def gather_queries(q):
    n = lax.axis_size("ctx")
    sems = pltpu.SemaphoreType.DMA((max(n - 1, 1),))
    return pl.pallas_call(
        gather_queries_kernel,
        out_shape=jax.ShapeDtypeStruct((n,) + q.shape, q.dtype),
        in_specs=vmem(1),
        out_specs=vmem(1)[0],
        scratch_shapes=[sems] * 4 + [pltpu.SemaphoreType.DMA],
        compiler_params=params(0),
        name="gather_queries",
    )(q)


def to_rows(block):
    shape = block.shape
    flat = (shape[0] * shape[1] * shape[2], shape[3])
    if shape[2] % 16 == 0:
        return block.reshape(flat)
    return block.astype(jnp.float32).reshape(flat).astype(block.dtype)


def attend_kernel(chunk, place_ref, q_ref, k_ref, v_ref, nk_ref, nv_ref, acc_ref, st_ref):
    ctx, heads, rows, width = q_ref.shape
    count = ctx * heads * rows
    q = to_rows(q_ref[...])
    scale = width ** (-0.5)
    cached = place_ref[0]
    new_start = place_ref[1]
    use_new = place_ref[2]
    keys = k_ref.shape[0]

    def scored(block, usable):
        s = lax.dot_general(block, q, (((1,), (1,)), ((), ())), preferred_element_type=jnp.float32)
        s = jnp.where(usable, s * scale, NEG)
        return s

    def update(state, s, usable, values):
        m, l, acc = state
        m_new = jnp.maximum(m, jnp.max(s, axis=0, keepdims=True))
        p = jnp.where(usable, jnp.exp(s - m_new), 0.0)
        alpha = jnp.exp(m - m_new)
        l = l * alpha + jnp.sum(p, axis=0, keepdims=True)
        pv = lax.dot_general(
            values, p.astype(jnp.bfloat16), (((0,), (0,)), ((), ())), preferred_element_type=jnp.float32
        )
        return m_new, l, acc * alpha + pv

    state = (
        jnp.full((1, count), NEG, jnp.float32),
        jnp.zeros((1, count), jnp.float32),
        jnp.zeros((width, count), jnp.float32),
    )
    for start in range(0, keys, chunk):
        usable = lax.broadcasted_iota(jnp.int32, (chunk, 1), 0) + start < cached
        s = scored(k_ref[start : start + chunk, :], usable)
        state = update(state, s, usable, v_ref[start : start + chunk, :])
    new_count = nk_ref.shape[0]
    lane = lax.broadcasted_iota(jnp.int32, (1, count), 1)
    token = lane // (heads * rows) * rows + lane % rows
    key_at = lax.broadcasted_iota(jnp.int32, (new_count, 1), 0) + new_start
    usable = (key_at <= token) & (use_new > 0)
    s = scored(nk_ref[...], usable)
    m, l, acc = update(state, s, usable, nv_ref[...])
    acc_ref[...] = acc[None]
    st_ref[...] = jnp.zeros(st_ref.shape, jnp.float32)
    st_ref[0, 0:1, :] = m
    st_ref[0, 1:2, :] = l


def attend(q_all, keys, values, new_keys, new_values, place):
    ctx, heads, rows, width = q_all.shape
    groups = keys.shape[1] // width
    size = heads // groups
    count = ctx * size * rows
    length = keys.shape[0]
    chunk = next(c for c in (512, 256, 128, length) if length % c == 0)
    column = lambda n: pl.BlockSpec((n, width), lambda g: (0, g))
    return pl.pallas_call(
        functools.partial(attend_kernel, chunk),
        grid=(groups,),
        out_shape=(
            jax.ShapeDtypeStruct((groups, width, count), jnp.float32),
            jax.ShapeDtypeStruct((groups, 8, count), jnp.float32),
        ),
        in_specs=[
            pl.BlockSpec(memory_space=pltpu.SMEM),
            pl.BlockSpec((ctx, size, rows, width), lambda g: (0, g, 0, 0)),
            column(length),
            column(length),
            column(new_keys.shape[0]),
            column(new_keys.shape[0]),
        ],
        out_specs=(
            pl.BlockSpec((1, width, count), lambda g: (g, 0, 0)),
            pl.BlockSpec((1, 8, count), lambda g: (g, 0, 0)),
        ),
        compiler_params=pltpu.CompilerParams(vmem_limit_bytes=VMEM_LIMIT),
        name="attend",
    )(place, q_all, keys, values, new_keys, new_values)


def merge_kernel(
    acc_ref, st_ref, o_ref,
    sib_st, chip_st, ctx_st, part, sib_part, mine_part, ctx_part,
    s_st, r_st, s_z, r_z, s_p, r_p, s_a, r_a, s_g, r_g, s_k, r_k,
):
    n, me, after, before = peers("ctx")
    k = lax.axis_index("khalf")
    sibling = {"khalf": 1 - k}
    meet([{"ctx": c} for c in after] + [sibling])
    groups, width, count = acc_ref.shape
    _, heads, rows, _ = part.shape
    size = heads // groups
    half = heads // 2

    def stat_of(ref, at=()):
        return ref[at + (slice(None), slice(0, 1))], ref[at + (slice(None), slice(1, 2))]

    def joined(a, b):
        m = jnp.maximum(a[0], b[0])
        return m, a[1] * jnp.exp(a[0] - m) + b[1] * jnp.exp(b[0] - m)

    copy = remote(st_ref, sib_st, s_st, r_st, sibling)
    copy.start()
    copy.wait()
    own = stat_of(st_ref)
    chip = joined(own, stat_of(sib_st))
    chip_st[...] = jnp.zeros(chip_st.shape, jnp.float32)
    chip_st[:, 0:1, :] = chip[0]
    chip_st[:, 1:2, :] = chip[1]
    copies = [
        remote(chip_st, ctx_st.at[i], s_z.at[i], r_z.at[i], {"ctx": c}) for i, c in enumerate(after)
    ]
    for copy in copies:
        copy.start()
    total = chip
    for i, copy in enumerate(copies):
        copy.wait()
        total = joined(total, stat_of(ctx_st, (i,)))
    factor = jnp.exp(own[0] - total[0]) / total[1]
    for g in range(groups):
        scaled = jnp.transpose(acc_ref[g] * factor[g])
        part[:, g * size : (g + 1) * size] = scaled.reshape(n, size, rows, width).astype(part.dtype)
    copy = remote(part.at[:, pl.ds((1 - k) * half, half)], sib_part, s_p, r_p, sibling)
    copy.start()
    copy.wait()
    for c in range(n):
        mine_part[c] = (
            part[c, pl.ds(k * half, half)].astype(jnp.float32) + sib_part[c].astype(jnp.float32)
        ).astype(part.dtype)
    copies = [
        remote(mine_part.at[c], ctx_part.at[i], s_a.at[i], r_a.at[i], {"ctx": c})
        for i, c in enumerate(after)
    ]
    for copy in copies:
        copy.start()
    summed = mine_part[me].astype(jnp.float32)
    for i, copy in enumerate(copies):
        copy.wait()
        summed = summed + ctx_part[i].astype(jnp.float32)
    mine = pl.ds(k * half, half)
    other = pl.ds((1 - k) * half, half)
    o_ref[me, mine] = summed.astype(o_ref.dtype)
    out = [
        remote(o_ref.at[me, mine], o_ref.at[me, mine], s_g.at[i], r_g.at[i], {"ctx": c})
        for i, c in enumerate(after)
    ]
    on = [remote(o_ref.at[me, mine], o_ref.at[me, mine], s_k.at[n - 1], r_k.at[n - 1], sibling)]
    for copy in out + on:
        copy.start()
    for i, c in enumerate(before):
        remote(o_ref.at[c, mine], o_ref.at[c, mine], s_g.at[i], r_g.at[i], sibling).wait_recv()
        copy = remote(o_ref.at[c, mine], o_ref.at[c, mine], s_k.at[i], r_k.at[i], sibling)
        copy.start()
        on.append(copy)
    for i, c in enumerate(before + [me]):
        remote(o_ref.at[c, other], o_ref.at[c, other], s_k.at[i], r_k.at[i], sibling).wait_recv()
    for copy in out + on:
        copy.wait_send()


def merge(acc, stats, heads, rows):
    n = lax.axis_size("ctx")
    width = acc.shape[1]
    f32 = lambda *shape: pltpu.VMEM(shape, jnp.float32)
    b16 = lambda *shape: pltpu.VMEM(shape, jnp.bfloat16)
    one = pltpu.SemaphoreType.DMA
    many = pltpu.SemaphoreType.DMA((n,))
    return pl.pallas_call(
        merge_kernel,
        out_shape=jax.ShapeDtypeStruct((n, heads, rows, width), jnp.bfloat16),
        in_specs=vmem(2),
        out_specs=vmem(1)[0],
        scratch_shapes=[
            f32(*stats.shape), f32(*stats.shape), f32(max(n - 1, 1), *stats.shape),
            b16(n, heads, rows, width), b16(n, heads // 2, rows, width),
            b16(n, heads // 2, rows, width), b16(max(n - 1, 1), heads // 2, rows, width),
            one, one, many, many, one, one, many, many, many, many, many, many,
        ],
        compiler_params=params(1),
        name="merge",
    )(acc, stats)


def norm_kernel(
    total_width, p_ref, r_ref, g_ref, h_ref, n_ref, got, sq, sq_got, s_x, r_x, s_q, r_q
):
    n, me, after, _ = peers("ctx")
    k = lax.axis_index("khalf")
    _, _, across, _ = peers("kv")
    partners = [{"ctx": c} for c in after]
    partners += [{"ctx": c, "khalf": 1 - k} for c in [me] + after]
    meet([{"kv": c} for c in across] + partners)
    copies = [
        remote(p_ref, got.at[i], s_x.at[i], r_x.at[i], {"kv": c}) for i, c in enumerate(across)
    ]
    for copy in copies:
        copy.start()
    summed = p_ref[...].astype(jnp.float32)
    for i, copy in enumerate(copies):
        copy.wait()
        summed = summed + got[i].astype(jnp.float32)
    hidden = (r_ref[...].astype(jnp.float32) + summed).astype(h_ref.dtype)
    h_ref[...] = hidden
    values = hidden.astype(jnp.float32)
    squares = values * values
    rows, columns = values.shape
    lanes = squares[:, 0:128]
    for at in range(128, columns, 128):
        lanes = lanes + squares[:, at : at + 128]
    row = jnp.sum(jnp.transpose(lanes), axis=0, keepdims=True)
    sq[...] = jnp.broadcast_to(row, sq.shape)
    copies = [
        remote(sq, sq_got.at[i], s_q.at[i], r_q.at[i], device) for i, device in enumerate(partners)
    ]
    for copy in copies:
        copy.start()
    total = row
    for i, copy in enumerate(copies):
        copy.wait()
        total = total + sq_got[i, 0:1, :]
    factor = lax.rsqrt(total / total_width + EPSILON)
    column = jnp.transpose(jnp.broadcast_to(factor, (128, rows)))[:, 0:1]
    n_ref[...] = (values * column * g_ref[...]).astype(n_ref.dtype)


def norm(partial, residual, gain, total_width):
    rows, columns = partial.shape
    devices = lax.axis_size("ctx") * 2
    across = lax.axis_size("kv")
    shape = jax.ShapeDtypeStruct((rows, columns), jnp.bfloat16)
    many = lambda n: pltpu.SemaphoreType.DMA((max(n, 1),))
    return pl.pallas_call(
        functools.partial(norm_kernel, total_width),
        out_shape=(shape, shape),
        in_specs=vmem(3),
        out_specs=tuple(vmem(2)),
        scratch_shapes=[
            pltpu.VMEM((max(across - 1, 1), rows, columns), jnp.bfloat16),
            pltpu.VMEM((8, rows), jnp.float32),
            pltpu.VMEM((devices - 1, 8, rows), jnp.float32),
            many(across - 1), many(across - 1), many(devices - 1), many(devices - 1),
        ],
        compiler_params=params(2),
        name="norm",
    )(partial, residual, gain)


def ffn_kernel(
    steps, x_ref, w_hbm, dn_hbm, h_ref, o_ref,
    x2, wbuf, dbuf, own, sib_out, sib_in, rs_in, rs_out, act, part, psend, got,
    w_sem, d_sem, s_s, s_r, r_s, r_r, a_s, a_r, f_s, f_r, x_s, x_r,
):
    n = lax.axis_size("ctx")
    c = lax.axis_index("ctx")
    k = lax.axis_index("khalf")
    _, kv, across, _ = peers("kv")
    sibling = {"khalf": 1 - k}
    left, right = {"ctx": lax.rem(c + n - 1, n)}, {"ctx": lax.rem(c + 1, n)}
    tokens, depth = x_ref.shape
    half = w_hbm.shape[2] // 2
    width = half // steps
    toks = tokens // 2
    w_rows = w_hbm.reshape(2 * depth, 2 * half)

    def column(h, s):
        return pl.multiple_of(h * half + s * width, 128)

    def load(s, j):
        h = k if j == 0 else 1 - k
        slot = lax.rem(s, 2)
        return pltpu.make_async_copy(
            w_rows.at[:, pl.ds(column(h, s), width)], wbuf.at[slot, j], w_sem.at[slot, j]
        )

    for s in range(min(2, steps)):
        load(s, 1).start()
        load(s, 0).start()
    down = pltpu.make_async_copy(dn_hbm, dbuf, d_sem)
    down.start()
    meet([left, right, sibling] + [{"kv": i} for i in across])

    row = lax.broadcasted_iota(jnp.int32, (128, 256), 0)
    lane = lax.broadcasted_iota(jnp.int32, (128, 256), 1)
    for s in range(2):
        spread = jnp.where(lane == 2 * row + s, 1.0, 0.0).astype(jnp.bfloat16)
        for b in range(depth // 128):
            x2[s * tokens : (s + 1) * tokens, b * 256 : (b + 1) * 256] = jnp.dot(
                x_ref[:, b * 128 : (b + 1) * 128], spread, preferred_element_type=jnp.float32
            ).astype(jnp.bfloat16)

    def product(s, j):
        load(s, j).wait()
        both = jnp.dot(x2[...], wbuf[lax.rem(s, 2), j], preferred_element_type=jnp.float32)
        return both.reshape(2, tokens, width)

    def to_sibling(s):
        return remote(sib_out.at[s], sib_in.at[s], s_s.at[s], s_r.at[s], sibling)

    def toward(d):
        return (left, right) if d == 0 else (right, left)

    def sums(d, s):
        return remote(rs_out.at[d, s], rs_in.at[d, s], r_s.at[d, s], r_r.at[d, s], toward(d)[0])

    def region(d, h, s):
        return act.at[pl.ds(d * toks, toks), pl.ds(column(h, s), width)]

    def onward(d, s):
        return remote(region(d, k, s), region(d, k, s), a_s.at[d, s], a_r.at[d, s], toward(d)[1])

    def to_other(d, h, s):
        return remote(region(d, h, s), region(d, h, s), f_s.at[d, s], f_r.at[d, s], sibling)

    distance = (c, n - 1 - c)

    def step(t, _):
        @pl.when(t < steps)
        def _():
            sib_out[t] = product(t, 1).astype(jnp.bfloat16)
            to_sibling(t).start()
            own[t] = product(t, 0)

            @pl.when(t + 2 < steps)
            def _():
                load(t + 2, 1).start()
                load(t + 2, 0).start()

        s = t - 1

        @pl.when((s >= 0) & (s < steps))
        def _():
            to_sibling(s).wait_recv()
            for d in range(2):
                rows = slice(d * toks, (d + 1) * toks)

                def total():
                    return own[s, :, rows, :] + sib_in[s, :, rows, :].astype(jnp.float32)

                @pl.when(distance[d] == n - 1)
                def _():
                    rs_out[d, s] = total().astype(jnp.bfloat16)
                    sums(d, s).start()

                @pl.when((distance[d] < n - 1) & (distance[d] > 0))
                def _():
                    sums(d, s).wait_recv()
                    rs_out[d, s] = (total() + rs_in[d, s].astype(jnp.float32)).astype(jnp.bfloat16)
                    sums(d, s).start()

                @pl.when(distance[d] == 0)
                def _():
                    sums(d, s).wait_recv()
                    both = total() + rs_in[d, s].astype(jnp.float32)
                    gate = both[0]
                    value = gate / (1.0 + jnp.exp(-gate)) * both[1]
                    act[rows, pl.ds(column(k, s), width)] = value.astype(jnp.bfloat16)
                    onward(d, s).start()
                    to_other(d, k, s).start()

        for d in range(2):
            at = t - 2 * distance[d] - 2

            @pl.when((distance[d] > 0) & (at >= 0) & (at < steps))
            def _():
                onward(d, at).wait_recv()

                @pl.when(distance[d] < n - 1)
                def _():
                    onward(d, at).start()

                to_other(d, k, at).start()

        return 0

    lax.fori_loop(0, steps + 2 * n, step, 0)

    def settle(s, _):
        to_sibling(s).wait_send()
        for d in range(2):
            to_other(d, 1 - k, s).wait_recv()
            to_other(d, k, s).wait_send()

            @pl.when(distance[d] > 0)
            def _():
                sums(d, s).wait_send()

            @pl.when(distance[d] < n - 1)
            def _():
                onward(d, s).wait_send()

        return 0

    lax.fori_loop(0, steps, settle, 0)
    down.wait()
    part[...] = jnp.zeros(part.shape, jnp.float32)
    deep = 2 * half // 7 if (2 * half) % (7 * 128) == 0 else 2 * half

    def add(i, _):
        at = pl.multiple_of(i * deep, 128)
        part[...] += jnp.dot(
            act[:, pl.ds(at, deep)], dbuf[pl.ds(at, deep), :], preferred_element_type=jnp.float32
        )
        return 0

    lax.fori_loop(0, 2 * half // deep, add, 0)
    rows = o_ref.shape[0]
    for b in range(tokens // rows):
        psend[b] = part[b * rows : (b + 1) * rows].astype(jnp.bfloat16)
    copies = [
        remote(psend.at[i], got.at[j], x_s.at[j], x_r.at[j], {"kv": i}) for j, i in enumerate(across)
    ]
    for copy in copies:
        copy.start()
    summed = psend[kv].astype(jnp.float32)
    for j, copy in enumerate(copies):
        copy.wait()
        summed = summed + got[j].astype(jnp.float32)
    o_ref[...] = (h_ref[kv].astype(jnp.float32) + summed).astype(o_ref.dtype)


def feed_forward(normed, gate_up, down_weight, hidden):
    tokens, depth = normed.shape
    half = gate_up.shape[2] // 2
    steps = next(s for s in (7, 8, 4, 2, 1) if half % (s * 128) == 0)
    width = half // steps
    columns = down_weight.shape[1]
    n = lax.axis_size("kv")
    rows = tokens // n
    b16 = lambda *shape: pltpu.VMEM(shape, jnp.bfloat16)
    f32 = lambda *shape: pltpu.VMEM(shape, jnp.float32)
    many = lambda *shape: pltpu.SemaphoreType.DMA(shape)
    anywhere = pl.BlockSpec(memory_space=pl.ANY)
    return pl.pallas_call(
        functools.partial(ffn_kernel, steps),
        out_shape=jax.ShapeDtypeStruct((rows, columns), jnp.bfloat16),
        in_specs=[vmem(1)[0], anywhere, anywhere, vmem(1)[0]],
        out_specs=vmem(1)[0],
        scratch_shapes=[
            b16(2 * tokens, 2 * depth), b16(2, 2, 2 * depth, width), b16(2 * half, columns),
            f32(steps, 2, tokens, width), b16(steps, 2, tokens, width), b16(steps, 2, tokens, width),
            b16(2, steps, 2, tokens // 2, width), b16(2, steps, 2, tokens // 2, width),
            b16(tokens, 2 * half), f32(tokens, columns), b16(n, rows, columns),
            b16(max(n - 1, 1), rows, columns),
            many(2, 2), many(), many(steps), many(steps), many(2, steps), many(2, steps),
            many(2, steps), many(2, steps), many(2, steps), many(2, steps),
            many(max(n - 1, 1)), many(max(n - 1, 1)),
        ],
        compiler_params=params(3),
        name="feed_forward",
    )(normed, gate_up, down_weight, hidden.reshape(n, rows, columns))


def on_device(
    queries,
    cache_keys,
    cache_values,
    new_keys,
    new_values,
    cache_blocks,
    residual,
    norm_gain,
    out_weight,
    gate_up,
    down_weight,
):
    rows = queries.shape[0]
    heads = queries.shape[1] // DH
    ctx = lax.axis_index("ctx")
    khalf = lax.axis_index("khalf")
    length = cache_keys.shape[0]
    start = (ctx * lax.axis_size("khalf") + khalf) * length
    place = jnp.stack(
        [cache_blocks[0] * BLOCK - start, ctx * rows, jnp.where(khalf == 0, 1, 0)]
    ).astype(jnp.int32)
    local_queries = queries.reshape(rows, heads, DH).transpose(1, 0, 2)
    q_all = gather_queries(local_queries)
    acc, stats = attend(q_all, cache_keys, cache_values, new_keys, new_values, place)
    attention = merge(acc, stats, heads, rows)
    tokens = attention.shape[0] * rows
    attention = attention.transpose(0, 2, 1, 3).reshape(tokens, heads * DH)
    partial_rows = jnp.dot(attention, out_weight, preferred_element_type=jnp.float32)
    total_width = out_weight.shape[1] * lax.axis_size("ctx") * lax.axis_size("khalf")
    hidden_state, normed = norm(
        partial_rows.astype(jnp.bfloat16), residual, norm_gain[None, :], total_width
    )
    return feed_forward(normed, gate_up, down_weight, hidden_state)


def solution(mesh):
    in_specs = (
        P(("groups", "ctx"), "kv"),
        P(("groups", "ctx", "khalf"), "kv"),
        P(("groups", "ctx", "khalf"), "kv"),
        P(("groups", "ctx"), "kv"),
        P(("groups", "ctx"), "kv"),
        P("groups"),
        P("groups", ("ctx", "khalf")),
        P(("ctx", "khalf")),
        P("kv", ("ctx", "khalf")),
        P(("ctx", "khalf"), None, "kv"),
        P("kv", ("ctx", "khalf")),
    )
    out_specs = P(("groups", "kv"), ("ctx", "khalf"))
    return jax.shard_map(
        on_device, mesh=mesh, in_specs=in_specs, out_specs=out_specs, check_vma=False
    )
```

```python
import functools

import jax
import jax.numpy as jnp
from jax import lax
from jax.experimental import pallas as pl
from jax.experimental.pallas import tpu as pltpu
from jax.sharding import PartitionSpec as P

HQ = 64
DH = 128
BLOCK = 128

NEG = -1e30
EPSILON = 1e-05
MESH = pl.DeviceIdType.MESH
VMEM_LIMIT = 56 * 1024 * 1024


def peers(axis):
    n = lax.axis_size(axis)
    me = lax.axis_index(axis)
    return n, me, [lax.rem(me + o, n) for o in range(1, n)], [
        lax.rem(me + n - o, n) for o in range(1, n)
    ]


def meet(devices):
    barrier = pltpu.get_barrier_semaphore()
    for device in devices:
        pl.semaphore_signal(barrier, inc=1, device_id=device, device_id_type=MESH)
    pl.semaphore_wait(barrier, len(devices))


def remote(src, dst, send, recv, device):
    return pltpu.make_async_remote_copy(
        src_ref=src, dst_ref=dst, send_sem=send, recv_sem=recv, device_id=device, device_id_type=MESH
    )


def vmem(count):
    return [pl.BlockSpec(memory_space=pltpu.VMEM)] * count


def params(collective_id):
    return pltpu.CompilerParams(
        collective_id=collective_id, has_side_effects=True, vmem_limit_bytes=VMEM_LIMIT
    )


def gather_line(o_ref, with_own, zs, zr, ks, kr):
    n, me, _, _ = peers("ctx")
    k = lax.axis_index("khalf")
    sibling = {"khalf": 1 - k}
    beside = ({"ctx": lax.rem(me + 1, n)}, {"ctx": lax.rem(me + n - 1, n)})
    has_next = (me < n - 1, me > 0)
    half = o_ref.shape[1] // 2
    mine, other = pl.ds(k * half, half), pl.ds((1 - k) * half, half)

    def pass_on(b, d):
        block = o_ref.at[b, mine]
        return remote(block, block, zs.at[d, b], zr.at[b], beside[d])

    def across(b, part):
        block = o_ref.at[b, part]
        return remote(block, block, ks.at[b], kr.at[b], sibling)

    for d in range(2):

        @pl.when(has_next[d])
        def _():
            pass_on(me, d).start()

    if with_own:
        across(me, mine).start()
    for hop in range(1, n):
        for d in range(2):
            b = me - hop if d == 0 else me + hop

            @pl.when((b >= 0) & (b < n))
            def _():
                pass_on(b, d).wait_recv()

                @pl.when(has_next[d])
                def _():
                    pass_on(b, d).start()

                across(b, mine).start()

    for b in range(n):

        @pl.when(jnp.logical_or(with_own, me != b))
        def _():
            across(b, other).wait_recv()
            across(b, mine).wait_send()

        for d in range(2):

            @pl.when(has_next[d] & ((b <= me) if d == 0 else (b >= me)))
            def _():
                pass_on(b, d).wait_send()


def gather_queries_kernel(q_ref, o_ref, zs, zr, ks, kr):
    n, me, _, _ = peers("ctx")
    meet(
        [
            {"ctx": lax.rem(me + 1, n)},
            {"ctx": lax.rem(me + n - 1, n)},
            {"khalf": 1 - lax.axis_index("khalf")},
        ]
    )
    o_ref[me] = q_ref[...]
    gather_line(o_ref, False, zs, zr, ks, kr)


def line_sems(n):
    sem = pltpu.SemaphoreType.DMA
    return [sem((2, n)), sem((n,)), sem((n,)), sem((n,))]


def gather_queries(q):
    n = lax.axis_size("ctx")
    return pl.pallas_call(
        gather_queries_kernel,
        out_shape=jax.ShapeDtypeStruct((n,) + q.shape, q.dtype),
        in_specs=vmem(1),
        out_specs=vmem(1)[0],
        scratch_shapes=line_sems(n),
        compiler_params=params(0),
        name="gather_queries",
    )(q)


def to_rows(block):
    shape = block.shape
    flat = (shape[0] * shape[1] * shape[2], shape[3])
    if shape[2] % 16 == 0:
        return block.reshape(flat)
    return block.astype(jnp.float32).reshape(flat).astype(block.dtype)


def attend_kernel(chunk, place_ref, q_ref, k_ref, v_ref, nk_ref, nv_ref, acc_ref, st_ref):
    ctx, heads, rows, width = q_ref.shape
    count = ctx * heads * rows
    q = to_rows(q_ref[...])
    scale = width ** (-0.5)
    cached = place_ref[0]
    new_start = place_ref[1]
    use_new = place_ref[2]
    keys = k_ref.shape[0]

    def scored(block, usable):
        s = lax.dot_general(block, q, (((1,), (1,)), ((), ())), preferred_element_type=jnp.float32)
        s = jnp.where(usable, s * scale, NEG)
        return s

    def update(state, s, usable, values):
        m, l, acc = state
        m_new = jnp.maximum(m, jnp.max(s, axis=0, keepdims=True))
        p = jnp.where(usable, jnp.exp(s - m_new), 0.0)
        alpha = jnp.exp(m - m_new)
        l = l * alpha + jnp.sum(p, axis=0, keepdims=True)
        pv = lax.dot_general(
            values, p.astype(jnp.bfloat16), (((0,), (0,)), ((), ())), preferred_element_type=jnp.float32
        )
        return m_new, l, acc * alpha + pv

    state = (
        jnp.full((1, count), NEG, jnp.float32),
        jnp.zeros((1, count), jnp.float32),
        jnp.zeros((width, count), jnp.float32),
    )
    for start in range(0, keys, chunk):
        usable = lax.broadcasted_iota(jnp.int32, (chunk, 1), 0) + start < cached
        s = scored(k_ref[start : start + chunk, :], usable)
        state = update(state, s, usable, v_ref[start : start + chunk, :])
    new_count = nk_ref.shape[0]
    lane = lax.broadcasted_iota(jnp.int32, (1, count), 1)
    token = lane // (heads * rows) * rows + lane % rows
    key_at = lax.broadcasted_iota(jnp.int32, (new_count, 1), 0) + new_start
    usable = (key_at <= token) & (use_new > 0)
    s = scored(nk_ref[...], usable)
    m, l, acc = update(state, s, usable, nv_ref[...])
    acc_ref[...] = acc[None]
    group = pl.program_id(0)
    st_ref[pl.ds(group, 1), :] = m
    st_ref[pl.ds(group + st_ref.shape[0] // 2, 1), :] = l


def attend(q_all, keys, values, new_keys, new_values, place):
    ctx, heads, rows, width = q_all.shape
    groups = keys.shape[1] // width
    size = heads // groups
    count = ctx * size * rows
    length = keys.shape[0]
    chunk = next(c for c in (512, 256, 128, length) if length % c == 0)
    column = lambda n: pl.BlockSpec((n, width), lambda g: (0, g))
    return pl.pallas_call(
        functools.partial(attend_kernel, chunk),
        grid=(groups,),
        out_shape=(
            jax.ShapeDtypeStruct((groups, width, count), jnp.float32),
            jax.ShapeDtypeStruct((2 * groups, count), jnp.float32),
        ),
        in_specs=[
            pl.BlockSpec(memory_space=pltpu.SMEM),
            pl.BlockSpec((ctx, size, rows, width), lambda g: (0, g, 0, 0)),
            column(length),
            column(length),
            column(new_keys.shape[0]),
            column(new_keys.shape[0]),
        ],
        out_specs=(
            pl.BlockSpec((1, width, count), lambda g: (g, 0, 0)),
            pl.BlockSpec((2 * groups, count), lambda g: (0, 0)),
        ),
        compiler_params=pltpu.CompilerParams(vmem_limit_bytes=VMEM_LIMIT),
        name="attend",
    )(place, q_all, keys, values, new_keys, new_values)


def merge_kernel(
    acc_ref, st_ref, o_ref,
    sib_st, chip_st, ctx_st, part, sib_part, mine_part, ctx_part,
    s_st, r_st, s_z, r_z, s_p, r_p, s_a, r_a, zs, zr, ks, kr,
):
    n, me, after, before = peers("ctx")
    k = lax.axis_index("khalf")
    sibling = {"khalf": 1 - k}
    meet([{"ctx": c} for c in after] + [sibling])
    groups, width, count = acc_ref.shape
    _, heads, rows, _ = part.shape
    size = heads // groups
    half = heads // 2

    def stat_of(ref, at=()):
        return ref[at + (slice(0, groups),)], ref[at + (slice(groups, 2 * groups),)]

    def joined(a, b):
        m = jnp.maximum(a[0], b[0])
        return m, a[1] * jnp.exp(a[0] - m) + b[1] * jnp.exp(b[0] - m)

    copy = remote(st_ref, sib_st, s_st, r_st, sibling)
    copy.start()
    copy.wait()
    own = stat_of(st_ref)
    chip = joined(own, stat_of(sib_st))
    chip_st[0:groups] = chip[0]
    chip_st[groups : 2 * groups] = chip[1]
    copies = [
        remote(chip_st, ctx_st.at[i], s_z.at[i], r_z.at[i], {"ctx": c}) for i, c in enumerate(after)
    ]
    for copy in copies:
        copy.start()
    total = chip
    for i, copy in enumerate(copies):
        copy.wait()
        total = joined(total, stat_of(ctx_st, (i,)))
    factor = jnp.exp(own[0] - total[0]) / total[1]
    for g in range(groups):
        scaled = jnp.transpose(acc_ref[g] * factor[g : g + 1])
        part[:, g * size : (g + 1) * size] = scaled.reshape(n, size, rows, width).astype(part.dtype)
    mine = pl.ds(k * half, half)
    other = pl.ds((1 - k) * half, half)
    swaps = [
        remote(part.at[c, other], sib_part.at[c], s_p.at[i], r_p.at[i], sibling)
        for i, c in enumerate(after + [me])
    ]
    meet_sums = []
    for copy in swaps:
        copy.start()
    for i, c in enumerate(after + [me]):
        swaps[i].wait_recv()
        summed = part[c, mine].astype(jnp.float32) + sib_part[c].astype(jnp.float32)
        if i < n - 1:
            mine_part[c] = summed.astype(part.dtype)
            copy = remote(mine_part.at[c], ctx_part.at[i], s_a.at[i], r_a.at[i], {"ctx": c})
            copy.start()
            meet_sums.append(copy)
    for i, copy in enumerate(meet_sums):
        copy.wait_recv()
        summed = summed + ctx_part[i].astype(jnp.float32)
    o_ref[me, mine] = summed.astype(o_ref.dtype)
    gather_line(o_ref, True, zs, zr, ks, kr)
    for copy in swaps + meet_sums:
        copy.wait_send()


def merge(acc, stats, heads, rows):
    n = lax.axis_size("ctx")
    width = acc.shape[1]
    f32 = lambda *shape: pltpu.VMEM(shape, jnp.float32)
    b16 = lambda *shape: pltpu.VMEM(shape, jnp.bfloat16)
    one = pltpu.SemaphoreType.DMA
    many = pltpu.SemaphoreType.DMA((n,))
    return pl.pallas_call(
        merge_kernel,
        out_shape=jax.ShapeDtypeStruct((n, heads, rows, width), jnp.bfloat16),
        in_specs=vmem(2),
        out_specs=vmem(1)[0],
        scratch_shapes=[
            f32(*stats.shape), f32(*stats.shape), f32(max(n - 1, 1), *stats.shape),
            b16(n, heads, rows, width), b16(n, heads // 2, rows, width),
            b16(n, heads // 2, rows, width), b16(max(n - 1, 1), heads // 2, rows, width),
            one, one, many, many, many, many, many, many, *line_sems(n),
        ],
        compiler_params=params(1),
        name="merge",
    )(acc, stats)


def norm_kernel(
    total_width, p_ref, r_ref, g_ref, h_ref, n_ref, got, sq, sq_got, s_x, r_x, s_q, r_q
):
    n, me, after, _ = peers("ctx")
    k = lax.axis_index("khalf")
    _, _, across, _ = peers("kv")
    partners = [{"ctx": c} for c in after]
    partners += [{"ctx": c, "khalf": 1 - k} for c in [me] + after]
    meet([{"kv": c} for c in across] + partners)
    copies = [
        remote(p_ref, got.at[i], s_x.at[i], r_x.at[i], {"kv": c}) for i, c in enumerate(across)
    ]
    for copy in copies:
        copy.start()
    summed = p_ref[...].astype(jnp.float32)
    for i, copy in enumerate(copies):
        copy.wait()
        summed = summed + got[i].astype(jnp.float32)
    hidden = (r_ref[...].astype(jnp.float32) + summed).astype(h_ref.dtype)
    h_ref[...] = hidden
    values = hidden.astype(jnp.float32)
    squares = values * values
    rows, columns = values.shape
    lanes = squares[:, 0:128]
    for at in range(128, columns, 128):
        lanes = lanes + squares[:, at : at + 128]
    row = jnp.sum(jnp.transpose(lanes), axis=0, keepdims=True)
    sq[...] = jnp.broadcast_to(row, sq.shape)
    copies = [
        remote(sq, sq_got.at[i], s_q.at[i], r_q.at[i], device) for i, device in enumerate(partners)
    ]
    for copy in copies:
        copy.start()
    total = row
    for i, copy in enumerate(copies):
        copy.wait()
        total = total + sq_got[i, 0:1, :]
    factor = lax.rsqrt(total / total_width + EPSILON)
    column = jnp.transpose(jnp.broadcast_to(factor, (128, rows)))[:, 0:1]
    n_ref[...] = (values * column * g_ref[...]).astype(n_ref.dtype)


def norm(partial, residual, gain, total_width):
    rows, columns = partial.shape
    devices = lax.axis_size("ctx") * 2
    across = lax.axis_size("kv")
    shape = jax.ShapeDtypeStruct((rows, columns), jnp.bfloat16)
    many = lambda n: pltpu.SemaphoreType.DMA((max(n, 1),))
    return pl.pallas_call(
        functools.partial(norm_kernel, total_width),
        out_shape=(shape, shape),
        in_specs=vmem(3),
        out_specs=tuple(vmem(2)),
        scratch_shapes=[
            pltpu.VMEM((max(across - 1, 1), rows, columns), jnp.bfloat16),
            pltpu.VMEM((8, rows), jnp.float32),
            pltpu.VMEM((devices - 1, 8, rows), jnp.float32),
            many(across - 1), many(across - 1), many(devices - 1), many(devices - 1),
        ],
        compiler_params=params(2),
        name="norm",
    )(partial, residual, gain)


def ffn_kernel(
    steps, b_ref, dn_hbm, h_ref, o_ref,
    dbuf, sib_in, rs_in, rs_out, act, part, psend, got,
    d_sem, s_s, s_r, r_s, r_r, a_s, a_r, f_s, f_r, x_s, x_r,
):
    n = lax.axis_size("ctx")
    c = lax.axis_index("ctx")
    k = lax.axis_index("khalf")
    _, kv, across, _ = peers("kv")
    sibling = {"khalf": 1 - k}
    left, right = {"ctx": lax.rem(c + n - 1, n)}, {"ctx": lax.rem(c + 1, n)}
    tokens = b_ref.shape[1]
    half = b_ref.shape[2] // 2
    width = half // steps
    toks = tokens // 2

    def column(h, s):
        return pl.multiple_of(h * half + s * width, 128)

    down = pltpu.make_async_copy(dn_hbm, dbuf, d_sem)
    down.start()
    meet([left, right, sibling] + [{"kv": i} for i in across])

    def to_sibling(s):
        return remote(
            b_ref.at[:, :, pl.ds(column(1 - k, s), width)], sib_in.at[s], s_s.at[s], s_r.at[s], sibling
        )

    def toward(d):
        return (left, right) if d == 0 else (right, left)

    def sums(d, s):
        return remote(rs_out.at[d, s], rs_in.at[d, s], r_s.at[d, s], r_r.at[d, s], toward(d)[0])

    def region(d, h, s):
        return act.at[pl.ds(d * toks, toks), pl.ds(column(h, s), width)]

    def onward(d, s):
        return remote(region(d, k, s), region(d, k, s), a_s.at[d, s], a_r.at[d, s], toward(d)[1])

    def to_other(d, h, s):
        return remote(region(d, h, s), region(d, h, s), f_s.at[d, s], f_r.at[d, s], sibling)

    distance = (c, n - 1 - c)

    for s in range(steps):
        to_sibling(s).start()

    def step(t, _):
        s = t

        @pl.when((s >= 0) & (s < steps))
        def _():
            to_sibling(s).wait_recv()
            for d in range(2):
                rows = slice(d * toks, (d + 1) * toks)

                def total():
                    own = b_ref[:, rows, pl.ds(column(k, s), width)].astype(jnp.float32)
                    return own + sib_in[s, :, rows, :].astype(jnp.float32)

                @pl.when(distance[d] == n - 1)
                def _():
                    rs_out[d, s] = total().astype(jnp.bfloat16)
                    sums(d, s).start()

                @pl.when((distance[d] < n - 1) & (distance[d] > 0))
                def _():
                    sums(d, s).wait_recv()
                    rs_out[d, s] = (total() + rs_in[d, s].astype(jnp.float32)).astype(jnp.bfloat16)
                    sums(d, s).start()

                @pl.when(distance[d] == 0)
                def _():
                    sums(d, s).wait_recv()
                    both = total() + rs_in[d, s].astype(jnp.float32)
                    gate = both[0]
                    value = gate / (1.0 + jnp.exp(-gate)) * both[1]
                    act[rows, pl.ds(column(k, s), width)] = value.astype(jnp.bfloat16)
                    onward(d, s).start()
                    to_other(d, k, s).start()

        for d in range(2):
            at = t - 2 * distance[d] - 1

            @pl.when((distance[d] > 0) & (at >= 0) & (at < steps))
            def _():
                onward(d, at).wait_recv()

                @pl.when(distance[d] < n - 1)
                def _():
                    onward(d, at).start()

                to_other(d, k, at).start()

        return 0

    lax.fori_loop(0, steps + 2 * n, step, 0)

    def settle(s, _):
        to_sibling(s).wait_send()
        for d in range(2):
            to_other(d, 1 - k, s).wait_recv()
            to_other(d, k, s).wait_send()

            @pl.when(distance[d] > 0)
            def _():
                sums(d, s).wait_send()

            @pl.when(distance[d] < n - 1)
            def _():
                onward(d, s).wait_send()

        return 0

    lax.fori_loop(0, steps, settle, 0)
    down.wait()
    part[...] = jnp.zeros(part.shape, jnp.float32)
    deep = 2 * half // 7 if (2 * half) % (7 * 128) == 0 else 2 * half

    def add(i, _):
        at = pl.multiple_of(i * deep, 128)
        part[...] += jnp.dot(
            act[:, pl.ds(at, deep)], dbuf[pl.ds(at, deep), :], preferred_element_type=jnp.float32
        )
        return 0

    lax.fori_loop(0, 2 * half // deep, add, 0)
    rows = o_ref.shape[0]
    for b in range(tokens // rows):
        psend[b] = part[b * rows : (b + 1) * rows].astype(jnp.bfloat16)
    copies = [
        remote(psend.at[i], got.at[j], x_s.at[j], x_r.at[j], {"kv": i}) for j, i in enumerate(across)
    ]
    for copy in copies:
        copy.start()
    summed = psend[kv].astype(jnp.float32)
    for j, copy in enumerate(copies):
        copy.wait()
        summed = summed + got[j].astype(jnp.float32)
    o_ref[...] = (h_ref[kv].astype(jnp.float32) + summed).astype(o_ref.dtype)


def feed_forward(both, down_weight, hidden):
    _, tokens, local_hidden = both.shape
    half = local_hidden // 2
    steps = next(s for s in (7, 8, 4, 2, 1) if half % (s * 128) == 0)
    width = half // steps
    columns = down_weight.shape[1]
    n = lax.axis_size("kv")
    rows = tokens // n
    b16 = lambda *shape: pltpu.VMEM(shape, jnp.bfloat16)
    f32 = lambda *shape: pltpu.VMEM(shape, jnp.float32)
    many = lambda *shape: pltpu.SemaphoreType.DMA(shape)
    anywhere = pl.BlockSpec(memory_space=pl.ANY)
    return pl.pallas_call(
        functools.partial(ffn_kernel, steps),
        out_shape=jax.ShapeDtypeStruct((rows, columns), jnp.bfloat16),
        in_specs=[vmem(1)[0], anywhere, vmem(1)[0]],
        out_specs=vmem(1)[0],
        scratch_shapes=[
            b16(2 * half, columns), b16(steps, 2, tokens, width),
            b16(2, steps, 2, tokens // 2, width), b16(2, steps, 2, tokens // 2, width),
            b16(tokens, 2 * half), f32(tokens, columns), b16(n, rows, columns),
            b16(max(n - 1, 1), rows, columns),
            many(), many(steps), many(steps), many(2, steps), many(2, steps),
            many(2, steps), many(2, steps), many(2, steps), many(2, steps),
            many(max(n - 1, 1)), many(max(n - 1, 1)),
        ],
        compiler_params=params(3),
        name="feed_forward",
    )(both, down_weight, hidden.reshape(n, rows, columns))


def on_device(
    queries,
    cache_keys,
    cache_values,
    new_keys,
    new_values,
    cache_blocks,
    residual,
    norm_gain,
    out_weight,
    gate_up,
    down_weight,
):
    rows = queries.shape[0]
    heads = queries.shape[1] // DH
    ctx = lax.axis_index("ctx")
    khalf = lax.axis_index("khalf")
    length = cache_keys.shape[0]
    start = (ctx * lax.axis_size("khalf") + khalf) * length
    place = jnp.stack(
        [cache_blocks[0] * BLOCK - start, ctx * rows, jnp.where(khalf == 0, 1, 0)]
    ).astype(jnp.int32)
    local_queries = queries.reshape(rows, heads, DH).transpose(1, 0, 2)
    q_all = gather_queries(local_queries)
    acc, stats = attend(q_all, cache_keys, cache_values, new_keys, new_values, place)
    attention = merge(acc, stats, heads, rows)
    tokens = attention.shape[0] * rows
    attention = attention.transpose(0, 2, 1, 3).reshape(tokens, heads * DH)
    partial_rows = jnp.dot(attention, out_weight, preferred_element_type=jnp.float32)
    total_width = out_weight.shape[1] * lax.axis_size("ctx") * lax.axis_size("khalf")
    hidden_state, normed = norm(
        partial_rows.astype(jnp.bfloat16), residual, norm_gain[None, :], total_width
    )
    both = jnp.einsum("tk,ksn->stn", normed, gate_up, preferred_element_type=jnp.float32)
    return feed_forward(both.astype(jnp.bfloat16), down_weight, hidden_state)


def solution(mesh):
    in_specs = (
        P(("groups", "ctx"), "kv"),
        P(("groups", "ctx", "khalf"), "kv"),
        P(("groups", "ctx", "khalf"), "kv"),
        P(("groups", "ctx"), "kv"),
        P(("groups", "ctx"), "kv"),
        P("groups"),
        P("groups", ("ctx", "khalf")),
        P(("ctx", "khalf")),
        P("kv", ("ctx", "khalf")),
        P(("ctx", "khalf"), None, "kv"),
        P("kv", ("ctx", "khalf")),
    )
    out_specs = P(("groups", "kv"), ("ctx", "khalf"))
    return jax.shard_map(
        on_device, mesh=mesh, in_specs=in_specs, out_specs=out_specs, check_vma=False
    )
```

```python
import functools

import jax
import jax.numpy as jnp
from jax import lax
from jax.experimental import pallas as pl
from jax.experimental.pallas import tpu as pltpu
from jax.sharding import PartitionSpec as P

HQ = 64
DH = 128
BLOCK = 128

NEG = -1e30
EPSILON = 1e-05
MESH = pl.DeviceIdType.MESH
VMEM_LIMIT = 56 * 1024 * 1024


def peers(axis):
    n = lax.axis_size(axis)
    me = lax.axis_index(axis)
    return n, me, [lax.rem(me + o, n) for o in range(1, n)], [
        lax.rem(me + n - o, n) for o in range(1, n)
    ]


def meet(devices):
    barrier = pltpu.get_barrier_semaphore()
    for device in devices:
        pl.semaphore_signal(barrier, inc=1, device_id=device, device_id_type=MESH)
    pl.semaphore_wait(barrier, len(devices))


def remote(src, dst, send, recv, device):
    return pltpu.make_async_remote_copy(
        src_ref=src, dst_ref=dst, send_sem=send, recv_sem=recv, device_id=device, device_id_type=MESH
    )


def vmem(count):
    return [pl.BlockSpec(memory_space=pltpu.VMEM)] * count


def params(collective_id):
    return pltpu.CompilerParams(
        collective_id=collective_id, has_side_effects=True, vmem_limit_bytes=VMEM_LIMIT
    )


def gather_line(o_ref, with_own, zs, zr, ks, kr):
    n, me, _, _ = peers("ctx")
    k = lax.axis_index("khalf")
    sibling = {"khalf": 1 - k}
    beside = ({"ctx": lax.rem(me + 1, n)}, {"ctx": lax.rem(me + n - 1, n)})
    has_next = (me < n - 1, me > 0)
    half = o_ref.shape[1] // 2
    mine, other = pl.ds(k * half, half), pl.ds((1 - k) * half, half)

    def pass_on(b, d):
        block = o_ref.at[b, mine]
        return remote(block, block, zs.at[d, b], zr.at[b], beside[d])

    def across(b, part):
        block = o_ref.at[b, part]
        return remote(block, block, ks.at[b], kr.at[b], sibling)

    for d in range(2):

        @pl.when(has_next[d])
        def _():
            pass_on(me, d).start()

    if with_own:
        across(me, mine).start()
    for hop in range(1, n):
        for d in range(2):
            b = me - hop if d == 0 else me + hop

            @pl.when((b >= 0) & (b < n))
            def _():
                pass_on(b, d).wait_recv()

                @pl.when(has_next[d])
                def _():
                    pass_on(b, d).start()

                across(b, mine).start()

    for b in range(n):

        @pl.when(jnp.logical_or(with_own, me != b))
        def _():
            across(b, other).wait_recv()
            across(b, mine).wait_send()

        for d in range(2):

            @pl.when(has_next[d] & ((b <= me) if d == 0 else (b >= me)))
            def _():
                pass_on(b, d).wait_send()


def line_sems(n):
    sem = pltpu.SemaphoreType.DMA
    return [sem((2, n)), sem((n,)), sem((n,)), sem((n,))]


def gather_queries_kernel(q_ref, o_ref, zs, zr, ks, kr, own):
    n, me, after, before = peers("ctx")
    k = lax.axis_index("khalf")
    sibling = {"khalf": 1 - k}
    meet([{"ctx": c} for c in after] + [sibling])
    half = q_ref.shape[0] // 2
    mine = pl.ds(k * half, half)
    other = pl.ds((1 - k) * half, half)
    out = [
        remote(q_ref.at[mine], o_ref.at[me, mine], zs.at[i], zr.at[i], {"ctx": c})
        for i, c in enumerate(after)
    ]
    for copy in out:
        copy.start()
    local = pltpu.make_async_copy(q_ref, o_ref.at[me], own)
    local.start()
    on = []
    for i, c in enumerate(before):
        remote(o_ref.at[c, mine], o_ref.at[c, mine], zs.at[i], zr.at[i], sibling).wait_recv()
        copy = remote(o_ref.at[c, mine], o_ref.at[c, mine], ks.at[i], kr.at[i], sibling)
        copy.start()
        on.append(copy)
    for i, c in enumerate(before):
        remote(o_ref.at[c, other], o_ref.at[c, other], ks.at[i], kr.at[i], sibling).wait_recv()
    local.wait()
    for copy in out + on:
        copy.wait_send()


def gather_queries(q):
    n = lax.axis_size("ctx")
    sems = pltpu.SemaphoreType.DMA((max(n - 1, 1),))
    return pl.pallas_call(
        gather_queries_kernel,
        out_shape=jax.ShapeDtypeStruct((n,) + q.shape, q.dtype),
        in_specs=vmem(1),
        out_specs=vmem(1)[0],
        scratch_shapes=[sems] * 4 + [pltpu.SemaphoreType.DMA],
        compiler_params=params(0),
        name="gather_queries",
    )(q)


def to_rows(block):
    shape = block.shape
    flat = (shape[0] * shape[1] * shape[2], shape[3])
    if shape[2] % 16 == 0:
        return block.reshape(flat)
    return block.astype(jnp.float32).reshape(flat).astype(block.dtype)


def attend_kernel(chunk, place_ref, q_ref, k_ref, v_ref, nk_ref, nv_ref, acc_ref, st_ref):
    ctx, heads, rows, width = q_ref.shape
    count = ctx * heads * rows
    q = to_rows(q_ref[...])
    scale = width ** (-0.5)
    cached = place_ref[0]
    new_start = place_ref[1]
    use_new = place_ref[2]
    keys = k_ref.shape[0]

    def scored(block, usable):
        s = lax.dot_general(block, q, (((1,), (1,)), ((), ())), preferred_element_type=jnp.float32)
        s = jnp.where(usable, s * scale, NEG)
        return s

    def update(state, s, usable, values):
        m, l, acc = state
        m_new = jnp.maximum(m, jnp.max(s, axis=0, keepdims=True))
        p = jnp.where(usable, jnp.exp(s - m_new), 0.0)
        alpha = jnp.exp(m - m_new)
        l = l * alpha + jnp.sum(p, axis=0, keepdims=True)
        pv = lax.dot_general(
            values, p.astype(jnp.bfloat16), (((0,), (0,)), ((), ())), preferred_element_type=jnp.float32
        )
        return m_new, l, acc * alpha + pv

    state = (
        jnp.full((1, count), NEG, jnp.float32),
        jnp.zeros((1, count), jnp.float32),
        jnp.zeros((width, count), jnp.float32),
    )
    for start in range(0, keys, chunk):
        usable = lax.broadcasted_iota(jnp.int32, (chunk, 1), 0) + start < cached
        s = scored(k_ref[start : start + chunk, :], usable)
        state = update(state, s, usable, v_ref[start : start + chunk, :])
    new_count = nk_ref.shape[0]
    lane = lax.broadcasted_iota(jnp.int32, (1, count), 1)
    token = lane // (heads * rows) * rows + lane % rows
    key_at = lax.broadcasted_iota(jnp.int32, (new_count, 1), 0) + new_start
    usable = (key_at <= token) & (use_new > 0)
    s = scored(nk_ref[...], usable)
    m, l, acc = update(state, s, usable, nv_ref[...])
    acc_ref[...] = acc[None]
    group = pl.program_id(0)
    st_ref[pl.ds(group, 1), :] = m
    st_ref[pl.ds(group + st_ref.shape[0] // 2, 1), :] = l


def attend(q_all, keys, values, new_keys, new_values, place):
    ctx, heads, rows, width = q_all.shape
    groups = keys.shape[1] // width
    size = heads // groups
    count = ctx * size * rows
    length = keys.shape[0]
    chunk = next(c for c in (512, 256, 128, length) if length % c == 0)
    column = lambda n: pl.BlockSpec((n, width), lambda g: (0, g))
    return pl.pallas_call(
        functools.partial(attend_kernel, chunk),
        grid=(groups,),
        out_shape=(
            jax.ShapeDtypeStruct((groups, width, count), jnp.float32),
            jax.ShapeDtypeStruct((2 * groups, count), jnp.float32),
        ),
        in_specs=[
            pl.BlockSpec(memory_space=pltpu.SMEM),
            pl.BlockSpec((ctx, size, rows, width), lambda g: (0, g, 0, 0)),
            column(length),
            column(length),
            column(new_keys.shape[0]),
            column(new_keys.shape[0]),
        ],
        out_specs=(
            pl.BlockSpec((1, width, count), lambda g: (g, 0, 0)),
            pl.BlockSpec((2 * groups, count), lambda g: (0, 0)),
        ),
        compiler_params=pltpu.CompilerParams(vmem_limit_bytes=VMEM_LIMIT),
        name="attend",
    )(place, q_all, keys, values, new_keys, new_values)


def merge_kernel(
    acc_ref, st_ref, o_ref,
    sib_st, chip_st, ctx_st, part, sib_part, mine_part, ctx_part,
    s_st, r_st, s_z, r_z, s_p, r_p, s_a, r_a, zs, zr, ks, kr,
):
    n, me, after, before = peers("ctx")
    k = lax.axis_index("khalf")
    sibling = {"khalf": 1 - k}
    meet([{"ctx": c} for c in after] + [sibling])
    groups, width, count = acc_ref.shape
    _, heads, rows, _ = part.shape
    size = heads // groups
    half = heads // 2

    def stat_of(ref, at=()):
        return ref[at + (slice(0, groups),)], ref[at + (slice(groups, 2 * groups),)]

    def joined(a, b):
        m = jnp.maximum(a[0], b[0])
        return m, a[1] * jnp.exp(a[0] - m) + b[1] * jnp.exp(b[0] - m)

    copy = remote(st_ref, sib_st, s_st, r_st, sibling)
    copy.start()
    copy.wait()
    own = stat_of(st_ref)
    chip = joined(own, stat_of(sib_st))
    chip_st[0:groups] = chip[0]
    chip_st[groups : 2 * groups] = chip[1]
    copies = [
        remote(chip_st, ctx_st.at[i], s_z.at[i], r_z.at[i], {"ctx": c}) for i, c in enumerate(after)
    ]
    for copy in copies:
        copy.start()
    total = chip
    for i, copy in enumerate(copies):
        copy.wait()
        total = joined(total, stat_of(ctx_st, (i,)))
    factor = jnp.exp(own[0] - total[0]) / total[1]
    for g in range(groups):
        scaled = jnp.transpose(acc_ref[g] * factor[g : g + 1])
        part[:, g * size : (g + 1) * size] = scaled.reshape(n, size, rows, width).astype(part.dtype)
    mine = pl.ds(k * half, half)
    other = pl.ds((1 - k) * half, half)
    swaps = [
        remote(part.at[c, other], sib_part.at[c], s_p.at[i], r_p.at[i], sibling)
        for i, c in enumerate(after + [me])
    ]
    meet_sums = []
    for copy in swaps:
        copy.start()
    for i, c in enumerate(after + [me]):
        swaps[i].wait_recv()
        summed = part[c, mine].astype(jnp.float32) + sib_part[c].astype(jnp.float32)
        if i < n - 1:
            mine_part[c] = summed.astype(part.dtype)
            copy = remote(mine_part.at[c], ctx_part.at[i], s_a.at[i], r_a.at[i], {"ctx": c})
            copy.start()
            meet_sums.append(copy)
    for i, copy in enumerate(meet_sums):
        copy.wait_recv()
        summed = summed + ctx_part[i].astype(jnp.float32)
    o_ref[me, mine] = summed.astype(o_ref.dtype)
    gather_line(o_ref, True, zs, zr, ks, kr)
    for copy in swaps + meet_sums:
        copy.wait_send()


def merge(acc, stats, heads, rows):
    n = lax.axis_size("ctx")
    width = acc.shape[1]
    f32 = lambda *shape: pltpu.VMEM(shape, jnp.float32)
    b16 = lambda *shape: pltpu.VMEM(shape, jnp.bfloat16)
    one = pltpu.SemaphoreType.DMA
    many = pltpu.SemaphoreType.DMA((n,))
    return pl.pallas_call(
        merge_kernel,
        out_shape=jax.ShapeDtypeStruct((n, heads, rows, width), jnp.bfloat16),
        in_specs=vmem(2),
        out_specs=vmem(1)[0],
        scratch_shapes=[
            f32(*stats.shape), f32(*stats.shape), f32(max(n - 1, 1), *stats.shape),
            b16(n, heads, rows, width), b16(n, heads // 2, rows, width),
            b16(n, heads // 2, rows, width), b16(max(n - 1, 1), heads // 2, rows, width),
            one, one, many, many, many, many, many, many, *line_sems(n),
        ],
        compiler_params=params(1),
        name="merge",
    )(acc, stats)


def norm_kernel(
    total_width, p_ref, r_ref, g_ref, h_ref, n_ref, got, sq, sq_got, s_x, r_x, s_q, r_q
):
    n, me, after, _ = peers("ctx")
    k = lax.axis_index("khalf")
    _, _, across, _ = peers("kv")
    partners = [{"ctx": c} for c in after]
    partners += [{"ctx": c, "khalf": 1 - k} for c in [me] + after]
    meet([{"kv": c} for c in across] + partners)
    copies = [
        remote(p_ref, got.at[i], s_x.at[i], r_x.at[i], {"kv": c}) for i, c in enumerate(across)
    ]
    for copy in copies:
        copy.start()
    summed = p_ref[...].astype(jnp.float32)
    for i, copy in enumerate(copies):
        copy.wait()
        summed = summed + got[i].astype(jnp.float32)
    hidden = (r_ref[...].astype(jnp.float32) + summed).astype(h_ref.dtype)
    h_ref[...] = hidden
    values = hidden.astype(jnp.float32)
    squares = values * values
    rows, columns = values.shape
    lanes = squares[:, 0:128]
    for at in range(128, columns, 128):
        lanes = lanes + squares[:, at : at + 128]
    row = jnp.sum(jnp.transpose(lanes), axis=0, keepdims=True)
    sq[...] = jnp.broadcast_to(row, sq.shape)
    copies = [
        remote(sq, sq_got.at[i], s_q.at[i], r_q.at[i], device) for i, device in enumerate(partners)
    ]
    for copy in copies:
        copy.start()
    total = row
    for i, copy in enumerate(copies):
        copy.wait()
        total = total + sq_got[i, 0:1, :]
    factor = lax.rsqrt(total / total_width + EPSILON)
    column = jnp.transpose(jnp.broadcast_to(factor, (128, rows)))[:, 0:1]
    n_ref[...] = (values * column * g_ref[...]).astype(n_ref.dtype)


def norm(partial, residual, gain, total_width):
    rows, columns = partial.shape
    devices = lax.axis_size("ctx") * 2
    across = lax.axis_size("kv")
    shape = jax.ShapeDtypeStruct((rows, columns), jnp.bfloat16)
    many = lambda n: pltpu.SemaphoreType.DMA((max(n, 1),))
    return pl.pallas_call(
        functools.partial(norm_kernel, total_width),
        out_shape=(shape, shape),
        in_specs=vmem(3),
        out_specs=tuple(vmem(2)),
        scratch_shapes=[
            pltpu.VMEM((max(across - 1, 1), rows, columns), jnp.bfloat16),
            pltpu.VMEM((8, rows), jnp.float32),
            pltpu.VMEM((devices - 1, 8, rows), jnp.float32),
            many(across - 1), many(across - 1), many(devices - 1), many(devices - 1),
        ],
        compiler_params=params(2),
        name="norm",
    )(partial, residual, gain)


def finish_kernel(p_ref, h_ref, o_ref, got, s_x, r_x):
    n, me, across, _ = peers("kv")
    meet([{"kv": c} for c in across])
    copies = [
        remote(p_ref.at[c], got.at[i], s_x.at[i], r_x.at[i], {"kv": c}) for i, c in enumerate(across)
    ]
    for copy in copies:
        copy.start()
    summed = p_ref[me].astype(jnp.float32)
    for i, copy in enumerate(copies):
        copy.wait()
        summed = summed + got[i].astype(jnp.float32)
    o_ref[...] = (h_ref[me].astype(jnp.float32) + summed).astype(o_ref.dtype)


def finish(partial, hidden):
    n = lax.axis_size("kv")
    rows, columns = partial.shape
    block = (n, rows // n, columns)
    many = pltpu.SemaphoreType.DMA((max(n - 1, 1),))
    return pl.pallas_call(
        finish_kernel,
        out_shape=jax.ShapeDtypeStruct(block[1:], jnp.bfloat16),
        in_specs=vmem(2),
        out_specs=vmem(1)[0],
        scratch_shapes=[pltpu.VMEM((max(n - 1, 1),) + block[1:], jnp.bfloat16), many, many],
        compiler_params=params(3),
        name="finish",
    )(partial.reshape(block), hidden.reshape(block))


def on_device(
    queries,
    cache_keys,
    cache_values,
    new_keys,
    new_values,
    cache_blocks,
    residual,
    norm_gain,
    out_weight,
    gate_up,
    down_weight,
):
    rows = queries.shape[0]
    heads = queries.shape[1] // DH
    ctx = lax.axis_index("ctx")
    khalf = lax.axis_index("khalf")
    length = cache_keys.shape[0]
    start = (ctx * lax.axis_size("khalf") + khalf) * length
    place = jnp.stack(
        [cache_blocks[0] * BLOCK - start, ctx * rows, jnp.where(khalf == 0, 1, 0)]
    ).astype(jnp.int32)
    local_queries = queries.reshape(rows, heads, DH).transpose(1, 0, 2)
    q_all = gather_queries(local_queries)
    acc, stats = attend(q_all, cache_keys, cache_values, new_keys, new_values, place)
    attention = merge(acc, stats, heads, rows)
    tokens = attention.shape[0] * rows
    attention = attention.transpose(0, 2, 1, 3).reshape(tokens, heads * DH)
    partial_rows = jnp.dot(attention, out_weight, preferred_element_type=jnp.float32)
    total_width = out_weight.shape[1] * lax.axis_size("ctx") * lax.axis_size("khalf")
    hidden_state, normed = norm(
        partial_rows.astype(jnp.bfloat16), residual, norm_gain[None, :], total_width
    )
    both = jnp.einsum("tk,ksn->tsn", normed, gate_up, preferred_element_type=jnp.float32)
    both = lax.psum_scatter(
        both.astype(jnp.bfloat16), ("ctx", "khalf"), scatter_dimension=0, tiled=True
    ).astype(jnp.float32)
    activated = (jax.nn.silu(both[:, 0]) * both[:, 1]).astype(jnp.bfloat16)
    partial_out = jnp.dot(
        lax.all_gather(activated, ("ctx", "khalf"), axis=0, tiled=True),
        down_weight,
        preferred_element_type=jnp.float32,
    )
    return finish(partial_out.astype(jnp.bfloat16), hidden_state)


def solution(mesh):
    in_specs = (
        P(("groups", "ctx"), "kv"),
        P(("groups", "ctx", "khalf"), "kv"),
        P(("groups", "ctx", "khalf"), "kv"),
        P(("groups", "ctx"), "kv"),
        P(("groups", "ctx"), "kv"),
        P("groups"),
        P("groups", ("ctx", "khalf")),
        P(("ctx", "khalf")),
        P("kv", ("ctx", "khalf")),
        P(("ctx", "khalf"), None, "kv"),
        P("kv", ("ctx", "khalf")),
    )
    out_specs = P(("groups", "kv"), ("ctx", "khalf"))
    return jax.shard_map(
        on_device, mesh=mesh, in_specs=in_specs, out_specs=out_specs, check_vma=False
    )
```
